512 devices in a mesh: dp: 32 (over x, y), mp: 16 (over z, core).
Axes of the slice: x: 4, y: 8, z: 8, core: 2. Of those that a mesh axis runs over, the one named last changes fastest.
Arguments:
- grad_parts: bfloat16 [32, 16384, 1024], P('dp', 'mp'), may hold values from -0.625 to 0.625
- owner: int32 [16], replicated, may hold values from 0 to 15, as said below
- slot: int32 [16], replicated, may hold values from 0 to 2
- left_stat: float32 [48, 1024, 1024], P('mp', 'dp'), may hold values from -6 to 6
- right_stat: float32 [48, 1024, 1024], P('mp', 'dp'), may hold values from -6 to 6
- left_root: bfloat16 [48, 1024, 1024], P('mp', 'dp'), as said below
- right_root: bfloat16 [48, 1024, 1024], P('mp', 'dp'), as said below
Outputs:
- new_left: float32 [48, 1024, 1024], P('mp', 'dp')
- new_right: float32 [48, 1024, 1024], P('mp', 'dp')
- update: bfloat16 [48, 1024, 1024], P('mp', 'dp')
The draws below stay inside these ranges and needn't reach their ends.
Inputs may be any that keep to these rules, and one draw needn't show every extreme that they name: No two blocks share an owner and a slot; some owner holds 3 blocks; owners 0 and 15 both hold blocks. `left_root`: each slot's matrix is symmetric. `right_root`: each slot's matrix is symmetric.
All inputs are finite; a program needn't handle non-finite values.
Results may differ from the reference program's by a relative error of at most 0.024.
Values may be sent and summed in bfloat16 or wider, within the bound.
No kernel may reach another device: no remote copies, remote signals or barrier semaphores. Data moves between devices by JAX's collectives and lax.ppermute only.
A program may use at most 64 MiB of HBM per device.

```python
import math
import jax
import jax.numpy as jnp
from jax import lax

B = 1024
SLOTS = 3
BLOCKS = 16
ROWS = 16384
N_DP = 32
N_MP = 16


def place_blocks(key):
    total_slots = N_MP * SLOTS
    at_end = jax.random.randint(jax.random.fold_in(key, 101), (), 0, 2).astype(jnp.int32)
    heavy = at_end * (N_MP - 1)
    other_end = (1 - at_end) * (N_MP - 1)
    other_slot = jax.random.randint(jax.random.fold_in(key, 104), (), 0, SLOTS).astype(jnp.int32)
    ranks = jax.random.permutation(jax.random.fold_in(key, 102), total_slots).astype(jnp.int32)
    pairs = jnp.arange(total_slots, dtype=jnp.int32)
    scores = jnp.where(pairs // SLOTS == heavy, pairs - total_slots, ranks)
    scores = jnp.where(pairs == other_end * SLOTS + other_slot, -total_slots - 1, scores)
    ordered = jnp.argsort(scores, stable=True).astype(jnp.int32)
    chosen = ordered[:N_MP]
    shuffle = jax.random.permutation(jax.random.fold_in(key, 103), N_MP).astype(jnp.int32)
    return jnp.zeros((N_MP,), jnp.int32).at[shuffle].set(chosen)


def symmetric_root(key, lowest, highest, spread):
    shape = (N_MP * SLOTS, B, B)
    noise = jax.random.normal(jax.random.fold_in(key, 1), shape, jnp.float32)
    paired = (noise + jnp.swapaxes(noise, 1, 2)) * (spread / math.sqrt(B))
    levels = jnp.exp(jax.random.uniform(jax.random.fold_in(key, 2), (N_MP * SLOTS, B, 1), jnp.float32, math.log(lowest), math.log(highest)))
    identity = jnp.eye(B, dtype=jnp.float32)
    return paired + levels * identity


def draw_owner(key, part):
    placed = place_blocks(key)
    return placed // SLOTS


def draw_slot(key, part):
    placed = place_blocks(key)
    return placed % SLOTS


def draw_left_root(key, part):
    key = jax.random.fold_in(key, 21)
    values = symmetric_root(key, 0.5, 2.0, 0.35)
    return values.astype(jnp.bfloat16)


def draw_right_root(key, part):
    key = jax.random.fold_in(key, 22)
    values = symmetric_root(key, 0.5, 2.0, 0.35)
    return values.astype(jnp.bfloat16)


def raised(values, own_key, source, target, parts, factor):
    def block_of(dim):
        return (jnp.arange(values.shape[dim]) // (values.shape[dim] // parts)).reshape((-1,) + (1,) * (values.ndim - 1 - dim))

    near = jax.random.permutation(own_key, parts)[block_of(target)]
    other_side = (block_of(target) + parts // 2) % parts
    return jnp.where((block_of(source) == near) | (block_of(source) == other_side), factor * values, values)


def block_levels(rng, extent, cuts, smallest, largest):
    factor_of = 1.0
    for position, parts in cuts:
        draws = jax.random.uniform(jax.random.fold_in(jax.random.fold_in(rng, 6), position), (parts,), jnp.float32, smallest / len(cuts), largest / len(cuts))
        factor_of = factor_of * jnp.repeat(jnp.exp(draws), extent[position] // parts).reshape((-1,) + (1,) * (len(extent) - 1 - position))
    return factor_of


def gaussian(own_key, dims, scale, reach, cuts=(), kind=jnp.bfloat16):
    factor_of = block_levels(own_key, dims, cuts, -0.22, 0.18) if cuts else 1.0
    values = jax.random.normal(own_key, dims, jnp.float32) * scale * factor_of
    return jnp.minimum(jnp.maximum(values, -reach), reach).astype(kind)


def bell_draw_with(rng, extent, scale, most, shards, heavy, kind=jnp.bfloat16):
    entries = scale * jax.random.normal(rng, extent, jnp.float32)
    if shards:
        entries = entries * block_levels(rng, extent, shards, -0.22, 0.18)
    return jnp.clip(raised(entries, jax.random.fold_in(rng, 3), *heavy), -most, most).astype(kind)


def setup_inputs(seed: int = 0) -> dict:
    keys = jax.random.split(jax.random.key(seed), 8)
    return {
        "grad_parts": bell_draw_with(keys[0], (N_DP, ROWS, B), 0.05, 0.625, ((0, 32), (1, 16)), (0, 1, 32, 2.75)),
        "owner": draw_owner(jax.random.fold_in(keys[7], 71), 0),
        "slot": draw_slot(jax.random.fold_in(keys[7], 71), 0),
        "left_stat": gaussian(keys[3], (N_MP * SLOTS, B, B), 1.0, 6.0, ((0, 16), (1, 32)), jnp.float32),
        "right_stat": gaussian(keys[4], (N_MP * SLOTS, B, B), 1.0, 6.0, ((0, 16), (1, 32)), jnp.float32),
        "left_root": draw_left_root(jax.random.fold_in(keys[7], 71), 0),
        "right_root": draw_right_root(jax.random.fold_in(keys[7], 71), 0),
    }


def reference(grad_parts, owner, slot, left_stat, right_stat, left_root, right_root):
    summed = jnp.sum(grad_parts.astype(jnp.float32), axis=0).astype(jnp.bfloat16)
    blocks = summed.reshape(BLOCKS, B, B)
    target = (owner * SLOTS + slot).astype(jnp.int32)

    def per_block(index):
        where_to = target[index]
        gradient = lax.dynamic_index_in_dim(blocks, index, 0, keepdims=False)
        left_old = lax.dynamic_index_in_dim(left_stat, where_to, 0, keepdims=False)
        right_old = lax.dynamic_index_in_dim(right_stat, where_to, 0, keepdims=False)
        left_inv = lax.dynamic_index_in_dim(left_root, where_to, 0, keepdims=False)
        right_inv = lax.dynamic_index_in_dim(right_root, where_to, 0, keepdims=False)
        left_next = 0.95 * left_old + 0.05 * jnp.dot(gradient, gradient.T, preferred_element_type=jnp.float32)
        right_next = 0.95 * right_old + 0.05 * jnp.dot(gradient.T, gradient, preferred_element_type=jnp.float32)
        mixed = jnp.dot(left_inv, gradient, preferred_element_type=jnp.float32).astype(jnp.bfloat16)
        result = jnp.dot(mixed, right_inv, preferred_element_type=jnp.float32).astype(jnp.bfloat16)
        return left_next, right_next, result

    lefts, rights, results = lax.map(per_block, jnp.arange(BLOCKS, dtype=jnp.int32))
    new_left = left_stat.at[target].set(lefts)
    new_right = right_stat.at[target].set(rights)
    update = jnp.zeros(left_root.shape, jnp.bfloat16).at[target].set(results)
    return (new_left, new_right, update)
```

```python
import jax
import jax.numpy as jnp
import numpy as np
from jax import lax
from jax.experimental import pallas as pl
from jax.experimental.pallas import tpu as pltpu
from jax.sharding import Mesh
from jax.sharding import PartitionSpec as P

NX, NY, NZ, NC = 4, 8, 8, 2
MP = NZ * NC
F32, BF16 = jnp.float32, jnp.bfloat16


def swap(value, axis):
    return lax.all_to_all(value, axis, 0, 0, tiled=True)


def share(value, axis, size):
    return swap(jnp.broadcast_to(value[None], (size,) + value.shape), axis)


def add_up(value):
    return jnp.sum(value.astype(F32), axis=0).astype(BF16)


def pick_kernel(index_ref, in_ref, out_ref):
    for place in range(out_ref.shape[0]):
        out_ref[place] = in_ref[index_ref[place]]


def pick(index, value):
    return pl.pallas_call(
        pick_kernel,
        out_shape=jax.ShapeDtypeStruct(index.shape + value.shape[1:], value.dtype),
        in_specs=[
            pl.BlockSpec(memory_space=pltpu.SMEM),
            pl.BlockSpec(memory_space=pltpu.VMEM),
        ],
        out_specs=pl.BlockSpec(memory_space=pltpu.VMEM),
    )(index, value)


def body(grad_parts, owner, slot, left_stat, right_stat, left_root, right_root):
    slots, rows, b = left_stat.shape
    ix_panel = b // NX
    here = lax.axis_index("z") * NC + lax.axis_index("c")
    iy = lax.axis_index("y")

    target = owner * slots + slot
    named = target[None, :] == jnp.arange(MP * slots, dtype=jnp.int32)[:, None]
    block_of = jnp.sum(jnp.where(named, jnp.arange(MP, dtype=jnp.int32)[None, :], 0), axis=1)
    filled = jnp.any(target[None, :] == (here * slots + jnp.arange(slots, dtype=jnp.int32))[:, None], axis=1)

    right_full = lax.all_gather(right_root, ("x", "y"), axis=1, tiled=True)

    which = slot[:, None, None]
    offered = jnp.where(
        which == 0, left_root[0][None], jnp.where(which == 1, left_root[1][None], left_root[2][None])
    )
    offered = swap(offered, ("z", "c"))
    root = lax.dynamic_index_in_dim(offered, owner[here], 0, keepdims=False)
    root = swap(root.reshape(rows, NX, ix_panel).transpose(1, 0, 2), "x").reshape(NX * rows, ix_panel)

    part = add_up(swap(grad_parts[0].reshape(NX, ix_panel, b), "x"))
    chunk = add_up(swap(part.reshape(NY, rows, b), "y"))

    panel = share(chunk, "y", NY).reshape(ix_panel, b)
    cross = share(chunk, "x", NX).reshape(NX * rows, b)

    gl = lax.dot_general(cross, panel, (((1,), (1,)), ((), ())), preferred_element_type=F32).astype(BF16)
    own = lax.dynamic_slice_in_dim(panel.reshape(ix_panel, NX, ix_panel), iy * rows, rows, 2)
    own = own.reshape(ix_panel, NX * rows)
    gr = lax.dot_general(own, panel, (((0,), (0,)), ((), ())), preferred_element_type=F32).astype(BF16)
    mx = jnp.dot(root, panel, preferred_element_type=F32).astype(BF16)

    gl = swap(gl.reshape(NX, rows, ix_panel), "x").transpose(1, 0, 2).reshape(rows, b)
    gr = add_up(swap(gr.reshape(NX, rows, b), "x"))
    mx = add_up(swap(mx.reshape(NX, rows, b), "x"))

    cut_rows, cut_cols = 3 * rows // NC, b // NZ
    items = jnp.concatenate([gl, gr, mx], axis=0)
    items = items.reshape(NC, cut_rows, NZ, cut_cols).transpose(2, 0, 1, 3).reshape(MP, cut_rows, cut_cols)
    items = pick(block_of, swap(items, ("z", "c")))
    items = swap(items.reshape(MP, slots, cut_rows, cut_cols), ("z", "c"))
    items = items.reshape(NZ, NC, slots, cut_rows, cut_cols).transpose(2, 1, 3, 0, 4).reshape(slots, 3 * rows, b)
    gl, gr, mx = items[:, :rows], items[:, rows : 2 * rows], items[:, 2 * rows :]

    keeper = filled[:, None, None]
    new_left = jnp.where(keeper, 0.95 * left_stat + 0.05 * gl.astype(F32), left_stat)
    new_right = jnp.where(keeper, 0.95 * right_stat + 0.05 * gr.astype(F32), right_stat)
    update = jnp.einsum("srn,snb->srb", mx, right_full, preferred_element_type=F32)
    update = jnp.where(keeper, update, 0.0).astype(BF16)
    return new_left, new_right, update


def solution(mesh):
    grid = Mesh(np.asarray(mesh.devices).reshape(NX, NY, NZ, NC), ("x", "y", "z", "c"))
    dp, mp = ("x", "y"), ("z", "c")
    state = P(mp, dp, None)
    return jax.shard_map(
        body,
        mesh=grid,
        in_specs=(P(dp, mp, None), P(), P(), state, state, state, state),
        out_specs=(state, state, state),
        check_vma=False,
    )
```

```python
import jax
import jax.numpy as jnp
import numpy as np
from jax import lax
from jax.experimental import pallas as pl
from jax.experimental.pallas import tpu as pltpu
from jax.sharding import Mesh
from jax.sharding import PartitionSpec as P

NX, NY, NZ, NC = 4, 8, 8, 2
MP = NZ * NC
F32, BF16 = jnp.float32, jnp.bfloat16


def swap(value, axis):
    return lax.all_to_all(value, axis, 0, 0, tiled=True)


def share(value, axis, size):
    return swap(jnp.broadcast_to(value[None], (size,) + value.shape), axis)


def add_up(value):
    return jnp.sum(value.astype(F32), axis=0).astype(BF16)


def pick_kernel(index_ref, in_ref, out_ref):
    for place in range(out_ref.shape[0]):
        out_ref[place] = in_ref[index_ref[place]]


def pick(index, value):
    return pl.pallas_call(
        pick_kernel,
        out_shape=jax.ShapeDtypeStruct(index.shape + value.shape[1:], value.dtype),
        in_specs=[
            pl.BlockSpec(memory_space=pltpu.SMEM),
            pl.BlockSpec(memory_space=pltpu.VMEM),
        ],
        out_specs=pl.BlockSpec(memory_space=pltpu.VMEM),
    )(index, value)


def body(grad_parts, owner, slot, left_stat, right_stat, left_root, right_root):
    slots, rows, b = left_stat.shape
    ix_panel = b // NX
    here = lax.axis_index("z") * NC + lax.axis_index("c")
    iy = lax.axis_index("y")

    target = owner * slots + slot
    named = target[None, :] == jnp.arange(MP * slots, dtype=jnp.int32)[:, None]
    block_of = jnp.sum(jnp.where(named, jnp.arange(MP, dtype=jnp.int32)[None, :], 0), axis=1)
    filled = jnp.any(target[None, :] == (here * slots + jnp.arange(slots, dtype=jnp.int32))[:, None], axis=1)

    left_all = lax.all_gather(left_root, ("z", "c"), axis=0)
    root = lax.dynamic_slice(left_all, (owner[here], slot[here], 0, 0), (1, 1, rows, b)).reshape(rows, NX, ix_panel)

    part = add_up(swap(grad_parts[0].reshape(NX, ix_panel, b), "x"))
    right_root, part = lax.optimization_barrier((right_root, part))
    right_full = lax.all_gather(right_root, ("x", "y"), axis=1, tiled=True)
    chunk = add_up(swap(part.reshape(NY, rows, b), "y"))

    panel = share(chunk, "y", NY).reshape(ix_panel, b)
    cross = jnp.broadcast_to(chunk[None], (NX, rows, b))
    cross = swap(jnp.concatenate([cross, root.transpose(1, 0, 2)], axis=2), "x")
    cross, root = cross[:, :, :b].reshape(NX * rows, b), cross[:, :, b:]

    own = lax.dynamic_slice_in_dim(panel.reshape(ix_panel, NX, ix_panel), iy * rows, rows, 2)
    own = own.transpose(1, 2, 0)
    lhs = jnp.concatenate([own, root], axis=1).reshape(2 * NX * rows, ix_panel)
    both = jnp.dot(lhs, panel, preferred_element_type=F32).astype(BF16).reshape(NX, 2 * rows, b)
    gl = lax.dot_general(cross, panel, (((1,), (1,)), ((), ())), preferred_element_type=F32).astype(BF16)
    half = ix_panel // 2
    gl = gl.reshape(NX, rows, 2, half).transpose(0, 2, 1, 3).reshape(NX, 2 * rows, half)
    both = swap(jnp.concatenate([both, gl], axis=2), "x")
    gl = both[:, :, b:].reshape(NX, 2, rows, half).transpose(2, 0, 1, 3).reshape(rows, b)
    both = add_up(both[:, :, :b])

    cut_rows, cut_cols = 3 * rows // NC, b // NZ
    items = jnp.concatenate([both, gl], axis=0)
    items = items.reshape(NC, cut_rows, NZ, cut_cols).transpose(2, 0, 1, 3).reshape(MP, cut_rows, cut_cols)
    items = pick(block_of, swap(items, ("z", "c")))
    items = swap(items.reshape(MP, slots, cut_rows, cut_cols), ("z", "c"))
    items = items.reshape(NZ, NC, slots, cut_rows, cut_cols).transpose(2, 1, 3, 0, 4).reshape(slots, 3 * rows, b)
    gr, mx, gl = items[:, :rows], items[:, rows : 2 * rows], items[:, 2 * rows :]

    keeper = filled[:, None, None]
    new_left = jnp.where(keeper, 0.95 * left_stat + 0.05 * gl.astype(F32), left_stat)
    new_right = jnp.where(keeper, 0.95 * right_stat + 0.05 * gr.astype(F32), right_stat)
    update = jnp.einsum("srn,snb->srb", mx, right_full, preferred_element_type=F32)
    update = jnp.where(keeper, update, 0.0).astype(BF16)
    return new_left, new_right, update


def solution(mesh):
    grid = Mesh(np.asarray(mesh.devices).reshape(NX, NY, NZ, NC), ("x", "y", "z", "c"))
    dp, mp = ("x", "y"), ("z", "c")
    state = P(mp, dp, None)
    return jax.shard_map(
        body,
        mesh=grid,
        in_specs=(P(dp, mp, None), P(), P(), state, state, state, state),
        out_specs=(state, state, state),
        check_vma=False,
    )
```

```python
import jax
import jax.numpy as jnp
import numpy as np
from jax import lax
from jax.experimental import pallas as pl
from jax.experimental.pallas import tpu as pltpu
from jax.sharding import Mesh
from jax.sharding import PartitionSpec as P

NX, NY, NZ, NC = 4, 8, 8, 2
NL = 2
NS = 2
MP = NZ * NC
F32, BF16 = jnp.float32, jnp.bfloat16


def swap(value, axis):
    return lax.all_to_all(value, axis, 0, 0, tiled=True)


def share(value, axis, size):
    return swap(jnp.broadcast_to(value[None], (size,) + value.shape), axis)


def add_up(value):
    return jnp.sum(value.astype(F32), axis=0).astype(BF16)


def pick_kernel(index_ref, in_ref, out_ref):
    for place in range(out_ref.shape[0]):
        out_ref[place] = in_ref[index_ref[place]]


def pick(index, value):
    return pl.pallas_call(
        pick_kernel,
        out_shape=jax.ShapeDtypeStruct(index.shape + value.shape[1:], value.dtype),
        in_specs=[
            pl.BlockSpec(memory_space=pltpu.SMEM),
            pl.BlockSpec(memory_space=pltpu.VMEM),
        ],
        out_specs=pl.BlockSpec(memory_space=pltpu.VMEM),
    )(index, value)


def body(grad_parts, owner, slot, left_stat, right_stat, left_root, right_root):
    slots, rows, b = left_stat.shape
    ix_panel = b // NX
    here = lax.axis_index(("zh", "zl", "c"))
    iy = lax.axis_index("yh") * NL + lax.axis_index("yl")

    target = owner * slots + slot
    named = target[None, :] == jnp.arange(MP * slots, dtype=jnp.int32)[:, None]
    block_of = jnp.sum(jnp.where(named, jnp.arange(MP, dtype=jnp.int32)[None, :], 0), axis=1)
    filled = jnp.any(target[None, :] == (here * slots + jnp.arange(slots, dtype=jnp.int32))[:, None], axis=1)

    roots = lax.all_gather(left_root, ("zh", "c"), axis=0)

    part = add_up(swap(grad_parts[0].reshape(NX * NL, ix_panel // NL, b), ("x", "yl")))
    right_root, part = lax.optimization_barrier((right_root, part))
    right_full = lax.all_gather(right_root, ("x", "yh", "yl"), axis=1, tiled=True)
    chunk = add_up(swap(part.reshape(NY // NL, rows, b), "yh"))

    panel = share(chunk, ("yl", "yh"), NY).reshape(ix_panel, b)

    def held(block):
        place = (owner[block] // (NS * NC)) * NC + owner[block] % NC
        return lax.dynamic_slice(roots, (place, slot[block], 0, 0), (1, 1, rows, b)).reshape(rows, b)

    root = lax.ppermute(held(here ^ NC), "zl", [(i, i ^ 1) for i in range(NS)])
    root = jnp.where(((owner[here] ^ here) & NC) == 0, held(here), root).reshape(rows, NX, ix_panel)
    panel, root = lax.optimization_barrier((panel, root))

    cross = jnp.broadcast_to(lax.dynamic_slice_in_dim(panel, iy * rows, rows, 0)[None], (NX, rows, b))
    cross = swap(jnp.concatenate([cross, root.transpose(1, 0, 2)], axis=2), "x")
    cross, root = cross[:, :, :b].reshape(NX * rows, b), cross[:, :, b:]

    own = lax.dynamic_slice_in_dim(panel.reshape(ix_panel, NX, ix_panel), iy * rows, rows, 2)
    own = own.transpose(1, 2, 0)
    lhs = jnp.concatenate([own, root], axis=1).reshape(2 * NX * rows, ix_panel)
    both = jnp.dot(lhs, panel, preferred_element_type=F32).astype(BF16).reshape(NX, 2 * rows, b)
    gl = lax.dot_general(cross, panel, (((1,), (1,)), ((), ())), preferred_element_type=F32).astype(BF16)
    half = ix_panel // 2
    gl = gl.reshape(NX, rows, 2, half).transpose(0, 2, 1, 3).reshape(NX, 2 * rows, half)
    both = swap(jnp.concatenate([both, gl], axis=2), "x")
    gl = both[:, :, b:].reshape(NX, 2, rows, half).transpose(2, 0, 1, 3).reshape(rows, b)
    both = add_up(both[:, :, :b])

    cut_rows, cut_cols = 3 * rows // NC, b // NZ
    items = jnp.concatenate([both, gl], axis=0)
    items = items.reshape(NC, cut_rows, NZ, cut_cols).transpose(2, 0, 1, 3).reshape(MP, cut_rows, cut_cols)
    items = pick(block_of, swap(items, ("zh", "zl", "c")))
    items = swap(items.reshape(MP, slots, cut_rows, cut_cols), ("zh", "zl", "c"))
    items = items.reshape(NZ, NC, slots, cut_rows, cut_cols).transpose(2, 1, 3, 0, 4).reshape(slots, 3 * rows, b)
    gr, mx, gl = items[:, :rows], items[:, rows : 2 * rows], items[:, 2 * rows :]

    keeper = filled[:, None, None]
    new_left = jnp.where(keeper, 0.95 * left_stat + 0.05 * gl.astype(F32), left_stat)
    new_right = jnp.where(keeper, 0.95 * right_stat + 0.05 * gr.astype(F32), right_stat)
    update = jnp.einsum("srn,snb->srb", mx, right_full, preferred_element_type=F32)
    update = jnp.where(keeper, update, 0.0).astype(BF16)
    return new_left, new_right, update


def solution(mesh):
    grid = Mesh(np.asarray(mesh.devices).reshape(NX, NY // NL, NL, NZ // NS, NS, NC), ("x", "yh", "yl", "zh", "zl", "c"))
    dp, mp = ("x", "yh", "yl"), ("zh", "zl", "c")
    state = P(mp, dp, None)
    return jax.shard_map(
        body,
        mesh=grid,
        in_specs=(P(dp, mp, None), P(), P(), state, state, state, state),
        out_specs=(state, state, state),
        check_vma=False,
    )
```

```python
import jax
import jax.numpy as jnp
import numpy as np
from jax import lax
from jax.experimental import pallas as pl
from jax.experimental.pallas import tpu as pltpu
from jax.sharding import Mesh
from jax.sharding import PartitionSpec as P

NX, NY, NZ, NC = 4, 8, 8, 2
NL = 2
NS = 2
MP = NZ * NC
F32, BF16 = jnp.float32, jnp.bfloat16


def swap(value, axis):
    return lax.all_to_all(value, axis, 0, 0, tiled=True)


def share(value, axis, size):
    return swap(jnp.broadcast_to(value[None], (size,) + value.shape), axis)


def add_up(value):
    return jnp.sum(value.astype(F32), axis=0).astype(BF16)


def pick_kernel(index_ref, in_ref, out_ref):
    for place in range(out_ref.shape[0]):
        out_ref[place] = in_ref[index_ref[place]]


def pick(index, value):
    value = pltpu.with_memory_space_constraint(value, pltpu.VMEM)
    return pl.pallas_call(
        pick_kernel,
        out_shape=jax.ShapeDtypeStruct(index.shape + value.shape[1:], value.dtype),
        in_specs=[
            pl.BlockSpec(memory_space=pltpu.SMEM),
            pl.BlockSpec(memory_space=pltpu.VMEM),
        ],
        out_specs=pl.BlockSpec(memory_space=pltpu.VMEM),
    )(index, value)


def body(grad_parts, owner, slot, left_stat, right_stat, left_root, right_root):
    slots, rows, b = left_stat.shape
    ix_panel = b // NX
    here = lax.axis_index(("zh", "zl", "c"))
    iy = lax.axis_index("yh") * NL + lax.axis_index("yl")

    target = owner * slots + slot
    named = target[None, :] == jnp.arange(MP * slots, dtype=jnp.int32)[:, None]
    block_of = jnp.sum(jnp.where(named, jnp.arange(MP, dtype=jnp.int32)[None, :], 0), axis=1)
    filled = jnp.any(target[None, :] == (here * slots + jnp.arange(slots, dtype=jnp.int32))[:, None], axis=1)

    roots = lax.all_gather(left_root, ("zh", "c"), axis=0)

    part = add_up(swap(grad_parts[0].reshape(NX * NL, ix_panel // NL, b), ("x", "yl")))
    right_root, part = lax.optimization_barrier((right_root, part))
    right_full = lax.all_gather(right_root, ("x", "yh", "yl"), axis=1, tiled=True)
    chunk = add_up(swap(part.reshape(NY // NL, rows, b), "yh"))

    panel = share(chunk, ("yl", "yh"), NY).reshape(ix_panel, b)

    def held(block):
        place = (owner[block] // (NS * NC)) * NC + owner[block] % NC
        return lax.dynamic_slice(roots, (place, slot[block], 0, 0), (1, 1, rows, b)).reshape(rows, b)

    own = held(here)
    root = lax.ppermute(held(here ^ NC), "zl", [(i, i ^ 1) for i in range(NS)])
    panel, own, root = lax.optimization_barrier((panel, own, root))
    root = jnp.where(((owner[here] ^ here) & NC) == 0, own, root).reshape(rows, NX, ix_panel)

    cross = jnp.broadcast_to(lax.dynamic_slice_in_dim(panel, iy * rows, rows, 0)[None], (NX, rows, b))
    cross = swap(jnp.concatenate([cross, root.transpose(1, 0, 2)], axis=2), "x")
    cross, root = cross[:, :, :b].reshape(NX * rows, b), cross[:, :, b:]

    own = lax.dynamic_slice_in_dim(panel.reshape(ix_panel, NX, ix_panel), iy * rows, rows, 2)
    own = own.transpose(1, 2, 0)
    lhs = jnp.concatenate([own, root], axis=1).reshape(2 * NX * rows, ix_panel)
    both = jnp.dot(lhs, panel, preferred_element_type=F32).astype(BF16).reshape(NX, 2 * rows, b)
    gl = lax.dot_general(cross, panel, (((1,), (1,)), ((), ())), preferred_element_type=F32).astype(BF16)
    half = ix_panel // 2
    gl = gl.reshape(NX, rows, 2, half).transpose(0, 2, 1, 3).reshape(NX, 2 * rows, half)
    both = swap(jnp.concatenate([both, gl], axis=2), "x")
    gl = both[:, :, b:].reshape(NX, 2, rows, half).transpose(2, 0, 1, 3).reshape(rows, b)
    both = add_up(both[:, :, :b])

    cut_rows, cut_cols = 3 * rows // NC, b // NZ
    items = jnp.concatenate([both, gl], axis=0)
    items = items.reshape(NC, cut_rows, NZ, cut_cols).transpose(2, 0, 1, 3).reshape(MP, cut_rows, cut_cols)
    items = pick(block_of, swap(items, ("zh", "zl", "c")))
    items = swap(items.reshape(MP, slots, cut_rows, cut_cols), ("zh", "zl", "c"))
    items = items.reshape(NZ, NC, slots, cut_rows, cut_cols).transpose(2, 1, 3, 0, 4).reshape(slots, 3 * rows, b)
    gr, mx, gl = items[:, :rows], items[:, rows : 2 * rows], items[:, 2 * rows :]

    keeper = filled[:, None, None]
    new_left = jnp.where(keeper, 0.95 * left_stat + 0.05 * gl.astype(F32), left_stat)
    new_right = jnp.where(keeper, 0.95 * right_stat + 0.05 * gr.astype(F32), right_stat)
    update = jnp.einsum("srn,snb->srb", mx, right_full, preferred_element_type=F32)
    update = jnp.where(keeper, update, 0.0).astype(BF16)
    return new_left, new_right, update


def solution(mesh):
    grid = Mesh(np.asarray(mesh.devices).reshape(NX, NY // NL, NL, NZ // NS, NS, NC), ("x", "yh", "yl", "zh", "zl", "c"))
    dp, mp = ("x", "yh", "yl"), ("zh", "zl", "c")
    state = P(mp, dp, None)
    return jax.shard_map(
        body,
        mesh=grid,
        in_specs=(P(dp, mp, None), P(), P(), state, state, state, state),
        out_specs=(state, state, state),
        check_vma=False,
    )
```

```python
import jax
import jax.numpy as jnp
import numpy as np
from jax import lax
from jax.experimental import pallas as pl
from jax.experimental.pallas import tpu as pltpu
from jax.sharding import Mesh
from jax.sharding import PartitionSpec as P

NX, NY, NZ, NC = 4, 8, 8, 2
NL = 2
NS = 2
MP = NZ * NC
F32, BF16 = jnp.float32, jnp.bfloat16


def swap(value, axis):
    return lax.all_to_all(value, axis, 0, 0, tiled=True)


def share(value, axis, size):
    return swap(jnp.broadcast_to(value[None], (size,) + value.shape), axis)


def add_up(value):
    return jnp.sum(value.astype(F32), axis=0).astype(BF16)


def pick_kernel(index_ref, in_ref, out_ref):
    for place in range(out_ref.shape[0]):
        out_ref[place] = in_ref[index_ref[place]]


def pick(index, value):
    value = pltpu.with_memory_space_constraint(value, pltpu.VMEM)
    return pl.pallas_call(
        pick_kernel,
        out_shape=jax.ShapeDtypeStruct(index.shape + value.shape[1:], value.dtype),
        in_specs=[
            pl.BlockSpec(memory_space=pltpu.SMEM),
            pl.BlockSpec(memory_space=pltpu.VMEM),
        ],
        out_specs=pl.BlockSpec(memory_space=pltpu.VMEM),
    )(index, value)


def body(grad_parts, owner, slot, left_stat, right_stat, left_root, right_root):
    slots, rows, b = left_stat.shape
    ix_panel = b // NX
    here = lax.axis_index(("zh", "zl", "c"))
    iy = lax.axis_index("yh") * NL + lax.axis_index("yl")

    target = owner * slots + slot
    named = target[None, :] == jnp.arange(MP * slots, dtype=jnp.int32)[:, None]
    block_of = jnp.sum(jnp.where(named, jnp.arange(MP, dtype=jnp.int32)[None, :], 0), axis=1)
    filled = jnp.any(target[None, :] == (here * slots + jnp.arange(slots, dtype=jnp.int32))[:, None], axis=1)

    roots = lax.all_gather(left_root, ("zh", "c"), axis=0)

    part = add_up(swap(grad_parts[0].reshape(NX * NL, ix_panel // NL, b), ("x", "yl")))
    right_root, part = lax.optimization_barrier((right_root, part))
    right_full = lax.all_gather(right_root, ("x", "yh", "yl"), axis=1, tiled=True)
    chunk = add_up(swap(part.reshape(NY // NL, rows, b), "yh"))

    panel = share(chunk, ("yl", "yh"), NY).reshape(ix_panel, b)

    bands = jnp.arange(MP, dtype=jnp.int32)
    place = ((owner >> 2) * NC + (owner & 1)) * slots + slot
    place = place + jnp.where(((owner ^ bands) & NC) == 0, 0, MP * slots)
    mine = jnp.sum(jnp.where(bands == here, place, 0))
    other = jnp.sum(jnp.where(bands == here ^ NC, place, 0))
    roots = roots.reshape(NZ // NS * NC * slots, rows, b)

    def held(place):
        place = jnp.where(place < MP * slots, place, place - MP * slots)
        return lax.dynamic_index_in_dim(roots, place, 0, keepdims=False)

    own = held(mine)
    root = lax.ppermute(held(other), "zl", [(i, i ^ 1) for i in range(NS)])
    panel, own, root = lax.optimization_barrier((panel, own, root))
    root = jnp.where(mine < MP * slots, own, root).reshape(rows, NX, ix_panel)

    cross = jnp.broadcast_to(lax.dynamic_slice_in_dim(panel, iy * rows, rows, 0)[None], (NX, rows, b))
    cross = swap(jnp.concatenate([cross, root.transpose(1, 0, 2)], axis=2), "x")
    cross, root = cross[:, :, :b].reshape(NX * rows, b), cross[:, :, b:]

    own = lax.dynamic_slice_in_dim(panel.reshape(ix_panel, NX, ix_panel), iy * rows, rows, 2)
    own = own.transpose(1, 2, 0)
    lhs = jnp.concatenate([own, root], axis=1).reshape(2 * NX * rows, ix_panel)
    both = jnp.dot(lhs, panel, preferred_element_type=F32).astype(BF16).reshape(NX, 2 * rows, b)
    gl = lax.dot_general(cross, panel, (((1,), (1,)), ((), ())), preferred_element_type=F32).astype(BF16)
    half = ix_panel // 2
    gl = gl.reshape(NX, rows, 2, half).transpose(0, 2, 1, 3).reshape(NX, 2 * rows, half)
    both = swap(jnp.concatenate([both, gl], axis=2), "x")
    gl = both[:, :, b:].reshape(NX, 2, rows, half).transpose(2, 0, 1, 3).reshape(rows, b)
    both = add_up(both[:, :, :b])

    cut_rows, cut_cols = 3 * rows // NC, b // NZ
    items = jnp.concatenate([both, gl], axis=0)
    items = items.reshape(NC, cut_rows, NZ, cut_cols).transpose(2, 0, 1, 3).reshape(MP, cut_rows, cut_cols)
    items = pick(block_of, swap(items, ("zh", "zl", "c")))
    items = swap(items.reshape(MP, slots, cut_rows, cut_cols), ("zh", "zl", "c"))
    items = items.reshape(NZ, NC, slots, cut_rows, cut_cols).transpose(2, 1, 3, 0, 4).reshape(slots, 3 * rows, b)
    gr, mx, gl = items[:, :rows], items[:, rows : 2 * rows], items[:, 2 * rows :]

    keeper = filled[:, None, None]
    new_left = jnp.where(keeper, 0.95 * left_stat + 0.05 * gl.astype(F32), left_stat)
    new_right = jnp.where(keeper, 0.95 * right_stat + 0.05 * gr.astype(F32), right_stat)
    update = jnp.einsum("srn,snb->srb", mx, right_full, preferred_element_type=F32)
    update = jnp.where(keeper, update, 0.0).astype(BF16)
    return new_left, new_right, update


def solution(mesh):
    grid = Mesh(np.asarray(mesh.devices).reshape(NX, NY // NL, NL, NZ // NS, NS, NC), ("x", "yh", "yl", "zh", "zl", "c"))
    dp, mp = ("x", "yh", "yl"), ("zh", "zl", "c")
    state = P(mp, dp, None)
    return jax.shard_map(
        body,
        mesh=grid,
        in_specs=(P(dp, mp, None), P(), P(), state, state, state, state),
        out_specs=(state, state, state),
        check_vma=False,
    )
```

```python
import jax
import jax.numpy as jnp
import numpy as np
from jax import lax
from jax.experimental import pallas as pl
from jax.experimental.pallas import tpu as pltpu
from jax.sharding import Mesh
from jax.sharding import PartitionSpec as P

NX, NY, NZ, NC = 4, 8, 8, 2
NL = 2
NS = 2
MP = NZ * NC
F32, BF16 = jnp.float32, jnp.bfloat16


def swap(value, axis):
    return lax.all_to_all(value, axis, 0, 0, tiled=True)


def share(value, axis, size):
    return swap(jnp.broadcast_to(value[None], (size,) + value.shape), axis)


def add_up(value):
    return jnp.sum(value.astype(F32), axis=0).astype(BF16)


def pick_kernel(index_ref, in_ref, out_ref):
    for place in range(out_ref.shape[0]):
        out_ref[place] = in_ref[index_ref[place]]


def pick(index, value):
    value = pltpu.with_memory_space_constraint(value, pltpu.VMEM)
    return pl.pallas_call(
        pick_kernel,
        out_shape=jax.ShapeDtypeStruct(index.shape + value.shape[1:], value.dtype),
        in_specs=[
            pl.BlockSpec(memory_space=pltpu.SMEM),
            pl.BlockSpec(memory_space=pltpu.VMEM),
        ],
        out_specs=pl.BlockSpec(memory_space=pltpu.VMEM),
    )(index, value)


def multiply_kernel(filled_ref, left_ref, right_ref, out_ref, held, arrived):
    parts = [(i, j) for i in range(held.shape[0]) for j in range(held.shape[1])]
    copies = [pltpu.make_async_copy(right_ref.at[i, j], held.at[i, j], arrived.at[i, j]) for i, j in parts]
    for copy in copies:
        copy.start()
    deep = held.shape[2]
    for i in range(held.shape[0]):
        total = None
        for j in range(held.shape[1]):
            copies[i * held.shape[1] + j].wait()
            term = jnp.dot(left_ref[i, :, j * deep : (j + 1) * deep], held[i, j], preferred_element_type=F32)
            total = term if total is None else total + term
        out_ref[i] = jnp.where(filled_ref[i] > 0, total, 0.0).astype(out_ref.dtype)


def multiply(filled, left, right, cuts):
    slots, rows, b = left.shape
    vmem = pl.BlockSpec(memory_space=pltpu.VMEM)
    return pl.pallas_call(
        multiply_kernel,
        out_shape=jax.ShapeDtypeStruct(left.shape, left.dtype),
        in_specs=[pl.BlockSpec(memory_space=pltpu.SMEM), vmem, pl.BlockSpec(memory_space=pl.ANY)],
        out_specs=vmem,
        scratch_shapes=[
            pltpu.VMEM((slots, cuts, b // cuts, b), right.dtype),
            pltpu.SemaphoreType.DMA((slots, cuts)),
        ],
        compiler_params=pltpu.CompilerParams(vmem_limit_bytes=60 << 20),
    )(filled.astype(jnp.int32), left, right.reshape(slots, cuts, b // cuts, b))


def body(grad_parts, owner, slot, left_stat, right_stat, left_root, right_root):
    slots, rows, b = left_stat.shape
    ix_panel = b // NX
    here = lax.axis_index(("zh", "zl", "c"))
    iy = lax.axis_index("yh") * NL + lax.axis_index("yl")

    target = owner * slots + slot
    named = target[None, :] == jnp.arange(MP * slots, dtype=jnp.int32)[:, None]
    block_of = jnp.sum(jnp.where(named, jnp.arange(MP, dtype=jnp.int32)[None, :], 0), axis=1)
    filled = jnp.any(target[None, :] == (here * slots + jnp.arange(slots, dtype=jnp.int32))[:, None], axis=1)

    roots = lax.all_gather(left_root, ("zh", "c"), axis=0)

    part = add_up(swap(grad_parts[0].reshape(NX * NL, ix_panel // NL, b), ("x", "yl")))
    right_root, part = lax.optimization_barrier((right_root, part))
    right_full = lax.all_gather(right_root, ("x", "yh", "yl"), axis=1, tiled=True)
    chunk = add_up(swap(part.reshape(NY // NL, rows, b), "yh"))

    panel = share(chunk, ("yl", "yh"), NY).reshape(ix_panel, b)

    bands = jnp.arange(MP, dtype=jnp.int32)
    place = ((owner >> 2) * NC + (owner & 1)) * slots + slot
    place = place + jnp.where(((owner ^ bands) & NC) == 0, 0, MP * slots)
    mine = jnp.sum(jnp.where(bands == here, place, 0))
    other = jnp.sum(jnp.where(bands == here ^ NC, place, 0))
    roots = roots.reshape(NZ // NS * NC * slots, rows, b)

    def held(place):
        place = jnp.where(place < MP * slots, place, place - MP * slots)
        return lax.dynamic_index_in_dim(roots, place, 0, keepdims=False)

    own = held(mine)
    root = lax.ppermute(held(other), "zl", [(i, i ^ 1) for i in range(NS)])
    panel, own, root = lax.optimization_barrier((panel, own, root))
    root = jnp.where(mine < MP * slots, own, root).reshape(rows, NX, ix_panel)

    cross = jnp.broadcast_to(lax.dynamic_slice_in_dim(panel, iy * rows, rows, 0)[None], (NX, rows, b))
    cross = swap(jnp.concatenate([cross, root.transpose(1, 0, 2)], axis=2), "x")
    cross, root = cross[:, :, :b].reshape(NX * rows, b), cross[:, :, b:]

    own = lax.dynamic_slice_in_dim(panel.reshape(ix_panel, NX, ix_panel), iy * rows, rows, 2)
    own = own.transpose(1, 2, 0)
    lhs = jnp.concatenate([own, root], axis=1).reshape(2 * NX * rows, ix_panel)
    both = jnp.dot(lhs, panel, preferred_element_type=F32).astype(BF16).reshape(NX, 2 * rows, b)
    gl = lax.dot_general(cross, panel, (((1,), (1,)), ((), ())), preferred_element_type=F32).astype(BF16)
    half = ix_panel // 2
    gl = gl.reshape(NX, rows, 2, half).transpose(0, 2, 1, 3).reshape(NX, 2 * rows, half)
    both = swap(jnp.concatenate([both, gl], axis=2), "x")
    gl = both[:, :, b:].reshape(NX, 2, rows, half).transpose(2, 0, 1, 3).reshape(rows, b)
    both = add_up(both[:, :, :b])

    cut_rows, cut_cols = 3 * rows // NC, b // NZ
    items = jnp.concatenate([both, gl], axis=0)
    items = items.reshape(NC, cut_rows, NZ, cut_cols).transpose(2, 0, 1, 3).reshape(MP, cut_rows, cut_cols)
    items = pick(block_of, swap(items, ("zh", "zl", "c")))
    items = swap(items.reshape(MP, slots, cut_rows, cut_cols), ("zh", "zl", "c"))
    items = items.reshape(NZ, NC, slots, cut_rows, cut_cols).transpose(2, 1, 3, 0, 4).reshape(slots, 3 * rows, b)
    gr, mx, gl = items[:, :rows], items[:, rows : 2 * rows], items[:, 2 * rows :]

    keeper = filled[:, None, None]
    new_left = jnp.where(keeper, 0.95 * left_stat + 0.05 * gl.astype(F32), left_stat)
    new_right = jnp.where(keeper, 0.95 * right_stat + 0.05 * gr.astype(F32), right_stat)
    update = multiply(filled, mx, right_full, 4)
    return new_left, new_right, update


def solution(mesh):
    grid = Mesh(np.asarray(mesh.devices).reshape(NX, NY // NL, NL, NZ // NS, NS, NC), ("x", "yh", "yl", "zh", "zl", "c"))
    dp, mp = ("x", "yh", "yl"), ("zh", "zl", "c")
    state = P(mp, dp, None)
    return jax.shard_map(
        body,
        mesh=grid,
        in_specs=(P(dp, mp, None), P(), P(), state, state, state, state),
        out_specs=(state, state, state),
        check_vma=False,
    )
```

```python
import jax
import jax.numpy as jnp
import numpy as np
from jax import lax
from jax.experimental import pallas as pl
from jax.experimental.pallas import tpu as pltpu
from jax.sharding import Mesh
from jax.sharding import PartitionSpec as P

NX, NY, NZ, NC = 4, 8, 8, 2
NL = 2
NS = 2
MP = NZ * NC
F32, BF16 = jnp.float32, jnp.bfloat16


def swap(value, axis):
    return lax.all_to_all(value, axis, 0, 0, tiled=True)


def share(value, axis, size):
    return swap(jnp.broadcast_to(value[None], (size,) + value.shape), axis)


def add_up(value):
    return jnp.sum(value.astype(F32), axis=0).astype(BF16)


def pick_kernel(index_ref, in_ref, out_ref):
    for place in range(out_ref.shape[0]):
        out_ref[place] = in_ref[index_ref[place]]


def pick(index, value):
    value = pltpu.with_memory_space_constraint(value, pltpu.VMEM)
    return pl.pallas_call(
        pick_kernel,
        out_shape=jax.ShapeDtypeStruct(index.shape + value.shape[1:], value.dtype),
        in_specs=[
            pl.BlockSpec(memory_space=pltpu.SMEM),
            pl.BlockSpec(memory_space=pltpu.VMEM),
        ],
        out_specs=pl.BlockSpec(memory_space=pltpu.VMEM),
    )(index, value)


def body(grad_parts, owner, slot, left_stat, right_stat, left_root, right_root):
    slots, rows, b = left_stat.shape
    ix_panel = b // NX
    here = lax.axis_index(("zh", "zl", "c"))
    iy = lax.axis_index("yh") * NL + lax.axis_index("yl")

    target = owner * slots + slot
    named = target[None, :] == jnp.arange(MP * slots, dtype=jnp.int32)[:, None]
    block_of = jnp.sum(jnp.where(named, jnp.arange(MP, dtype=jnp.int32)[None, :], 0), axis=1)
    filled = jnp.any(target[None, :] == (here * slots + jnp.arange(slots, dtype=jnp.int32))[:, None], axis=1)

    roots = lax.all_gather(left_root, ("zh", "c"), axis=0)

    part = add_up(swap(grad_parts[0].reshape(NX * NL, ix_panel // NL, b), ("x", "yl")))
    right_root, part = lax.optimization_barrier((right_root, part))
    right_full = lax.all_gather(right_root, ("x", "yh", "yl"), axis=1, tiled=True)
    chunk = add_up(swap(part.reshape(NY // NL, rows, b), "yh"))

    panel = share(chunk, ("yl", "yh"), NY).reshape(ix_panel, b)

    bands = jnp.arange(MP, dtype=jnp.int32)
    place = ((owner >> 2) * NC + (owner & 1)) * slots + slot
    place = place + jnp.where(((owner ^ bands) & NC) == 0, 0, MP * slots)
    mine = jnp.sum(jnp.where(bands == here, place, 0))
    other = jnp.sum(jnp.where(bands == here ^ NC, place, 0))
    roots = roots.reshape(NZ // NS * NC * slots, rows, b)

    def held(place):
        place = jnp.where(place < MP * slots, place, place - MP * slots)
        return lax.dynamic_index_in_dim(roots, place, 0, keepdims=False)

    own = held(mine)
    root = lax.ppermute(held(other), "zl", [(i, i ^ 1) for i in range(NS)])
    panel, own, root = lax.optimization_barrier((panel, own, root))
    root = jnp.where(mine < MP * slots, own, root).reshape(rows, NX, ix_panel)

    cross = jnp.broadcast_to(lax.dynamic_slice_in_dim(panel, iy * rows, rows, 0)[None], (NX, rows, b))
    cross = swap(jnp.concatenate([cross, root.transpose(1, 0, 2)], axis=2), "x")
    cross, root = cross[:, :, :b].reshape(NX * rows, b), cross[:, :, b:]

    own = lax.dynamic_slice_in_dim(panel.reshape(ix_panel, NX, ix_panel), iy * rows, rows, 2)
    own = own.transpose(1, 2, 0)
    lhs = jnp.concatenate([own, root], axis=1).reshape(2 * NX * rows, ix_panel)
    both = jnp.dot(lhs, panel, preferred_element_type=F32).astype(BF16).reshape(NX, 2 * rows, b)
    gl = lax.dot_general(cross, panel, (((1,), (1,)), ((), ())), preferred_element_type=F32).astype(BF16)
    half = ix_panel // 2
    gl = gl.reshape(NX, rows, 2, half).transpose(0, 2, 1, 3).reshape(NX, 2 * rows, half)
    both = swap(jnp.concatenate([both, gl], axis=2), "x")
    gl = both[:, :, b:].reshape(NX, 2, rows, half).transpose(2, 0, 1, 3).reshape(rows, b)
    both = add_up(both[:, :, :b])

    cut_rows, cut_cols = 3 * rows // NC, b // NZ
    items = jnp.concatenate([both, gl], axis=0)
    items = items.reshape(NC, cut_rows, NZ, cut_cols).transpose(2, 0, 1, 3).reshape(MP, cut_rows, cut_cols)
    items = pick(block_of, swap(items, ("zh", "zl", "c")))
    items = swap(items.reshape(MP, slots, cut_rows, cut_cols), ("zh", "zl", "c"))
    items = items.reshape(NZ, NC, slots, cut_rows, cut_cols).transpose(2, 1, 3, 0, 4).reshape(slots, 3 * rows, b)
    gr, mx, gl = items[:, :rows], items[:, rows : 2 * rows], items[:, 2 * rows :]

    keeper = filled[:, None, None]
    new_left = jnp.where(keeper, 0.95 * left_stat + 0.05 * gl.astype(F32), left_stat)
    new_right = jnp.where(keeper, 0.95 * right_stat + 0.05 * gr.astype(F32), right_stat)
    update = jnp.stack(
        [jnp.dot(mx[i], right_full[i], preferred_element_type=F32) for i in range(slots)]
    )
    update = jnp.where(keeper, update, 0.0).astype(BF16)
    return new_left, new_right, update


def solution(mesh):
    grid = Mesh(np.asarray(mesh.devices).reshape(NX, NY // NL, NL, NZ // NS, NS, NC), ("x", "yh", "yl", "zh", "zl", "c"))
    dp, mp = ("x", "yh", "yl"), ("zh", "zl", "c")
    state = P(mp, dp, None)
    return jax.shard_map(
        body,
        mesh=grid,
        in_specs=(P(dp, mp, None), P(), P(), state, state, state, state),
        out_specs=(state, state, state),
        check_vma=False,
    )
```

```python
import jax
import jax.numpy as jnp
import numpy as np
from jax import lax
from jax.experimental import pallas as pl
from jax.experimental.pallas import tpu as pltpu
from jax.sharding import Mesh
from jax.sharding import PartitionSpec as P

NX, NY, NZ, NC = 4, 8, 8, 2
NL = 2
NS = 2
MP = NZ * NC
F32, BF16 = jnp.float32, jnp.bfloat16


def swap(value, axis):
    return lax.all_to_all(value, axis, 0, 0, tiled=True)


def share(value, axis, size):
    return swap(jnp.broadcast_to(value[None], (size,) + value.shape), axis)


def add_up(value):
    return jnp.sum(value.astype(F32), axis=0).astype(BF16)


def pick_kernel(index_ref, in_ref, out_ref):
    for place in range(out_ref.shape[0]):
        out_ref[place] = in_ref[index_ref[place]]


def pick(index, value):
    value = pltpu.with_memory_space_constraint(value, pltpu.VMEM)
    return pl.pallas_call(
        pick_kernel,
        out_shape=jax.ShapeDtypeStruct(index.shape + value.shape[1:], value.dtype),
        in_specs=[
            pl.BlockSpec(memory_space=pltpu.SMEM),
            pl.BlockSpec(memory_space=pltpu.VMEM),
        ],
        out_specs=pl.BlockSpec(memory_space=pltpu.VMEM),
    )(index, value)


def body(grad_parts, owner, slot, left_stat, right_stat, left_root, right_root):
    slots, rows, b = left_stat.shape
    ix_panel = b // NX
    here = lax.axis_index(("zh", "zl", "c"))
    iy = lax.axis_index("yh") * NL + lax.axis_index("yl")

    target = owner * slots + slot
    named = target[None, :] == jnp.arange(MP * slots, dtype=jnp.int32)[:, None]
    block_of = jnp.sum(jnp.where(named, jnp.arange(MP, dtype=jnp.int32)[None, :], 0), axis=1)
    filled = jnp.any(target[None, :] == (here * slots + jnp.arange(slots, dtype=jnp.int32))[:, None], axis=1)

    roots = lax.all_gather(left_root, ("c", "zh"), axis=0)

    part = add_up(swap(grad_parts[0].reshape(NX * NL, ix_panel // NL, b), ("x", "yl")))
    right_root, part = lax.optimization_barrier((right_root, part))
    right_full = lax.all_gather(right_root, ("x", "yh", "yl"), axis=1, tiled=True)
    chunk = add_up(swap(part.reshape(NY // NL, rows, b), "yh"))

    panel = share(chunk, ("yl", "yh"), NY).reshape(ix_panel, b)

    bands = jnp.arange(MP, dtype=jnp.int32)
    place = ((owner & 1) * (NZ // NS) + (owner >> 2)) * slots + slot
    place = place + jnp.where(((owner ^ bands) & NC) == 0, 0, MP * slots)
    mine = jnp.sum(jnp.where(bands == here, place, 0))
    other = jnp.sum(jnp.where(bands == here ^ NC, place, 0))
    roots = roots.reshape(NZ // NS * NC * slots, rows, b)

    def held(place):
        place = jnp.where(place < MP * slots, place, place - MP * slots)
        return lax.dynamic_index_in_dim(roots, place, 0, keepdims=False)

    own = held(mine)
    root = lax.ppermute(held(other), "zl", [(i, i ^ 1) for i in range(NS)])
    panel, own, root = lax.optimization_barrier((panel, own, root))
    root = jnp.where(mine < MP * slots, own, root).reshape(rows, NX, ix_panel)

    cross = jnp.broadcast_to(lax.dynamic_slice_in_dim(panel, iy * rows, rows, 0)[None], (NX, rows, b))
    cross = swap(jnp.concatenate([cross, root.transpose(1, 0, 2)], axis=2), "x")
    cross, root = cross[:, :, :b].reshape(NX * rows, b), cross[:, :, b:]

    own = lax.dynamic_slice_in_dim(panel.reshape(ix_panel, NX, ix_panel), iy * rows, rows, 2)
    own = own.transpose(1, 2, 0)
    lhs = jnp.concatenate([own, root], axis=1).reshape(2 * NX * rows, ix_panel)
    both = jnp.dot(lhs, panel, preferred_element_type=F32).astype(BF16).reshape(NX, 2 * rows, b)
    gl = lax.dot_general(cross, panel, (((1,), (1,)), ((), ())), preferred_element_type=F32).astype(BF16)
    half = ix_panel // 2
    gl = gl.reshape(NX, rows, 2, half).transpose(0, 2, 1, 3).reshape(NX, 2 * rows, half)
    both = swap(jnp.concatenate([both, gl], axis=2), "x")
    gl = both[:, :, b:].reshape(NX, 2, rows, half).transpose(2, 0, 1, 3).reshape(rows, b)
    both = add_up(both[:, :, :b])

    cut_rows, cut_cols = 3 * rows // NC, b // NZ
    items = jnp.concatenate([both, gl], axis=0)
    items = items.reshape(NC, cut_rows, NZ, cut_cols).transpose(2, 0, 1, 3).reshape(MP, cut_rows, cut_cols)
    items = pick(block_of, swap(items, ("zh", "zl", "c")))
    items = swap(items.reshape(MP, slots, cut_rows, cut_cols), ("zh", "zl", "c"))
    items = items.reshape(NZ, NC, slots, cut_rows, cut_cols).transpose(2, 1, 3, 0, 4).reshape(slots, 3 * rows, b)
    gr, mx, gl = items[:, :rows], items[:, rows : 2 * rows], items[:, 2 * rows :]

    keeper = filled[:, None, None]
    new_left = jnp.where(keeper, 0.95 * left_stat + 0.05 * gl.astype(F32), left_stat)
    new_right = jnp.where(keeper, 0.95 * right_stat + 0.05 * gr.astype(F32), right_stat)
    update = jnp.einsum("srn,snb->srb", mx, right_full, preferred_element_type=F32)
    update = jnp.where(keeper, update, 0.0).astype(BF16)
    return new_left, new_right, update


def solution(mesh):
    grid = Mesh(np.asarray(mesh.devices).reshape(NX, NY // NL, NL, NZ // NS, NS, NC), ("x", "yh", "yl", "zh", "zl", "c"))
    dp, mp = ("x", "yh", "yl"), ("zh", "zl", "c")
    state = P(mp, dp, None)
    return jax.shard_map(
        body,
        mesh=grid,
        in_specs=(P(dp, mp, None), P(), P(), state, state, state, state),
        out_specs=(state, state, state),
        check_vma=False,
    )
```
